32 devices in a mesh: groups: 2 (over y), fsdp: 4 (over z), tp: 4 (over x, core).
Axes of the slice: x: 2, y: 2, z: 4, core: 2. Of those that a mesh axis runs over, the one named last changes fastest.
Arguments:
- tokens: bfloat16 [1024, 4096], P(('groups', 'fsdp')), parts along dimension 0, may hold values from -16.15 to 16.15
- query_key_value_weight: bfloat16 [4096, 8, 1280], P('fsdp', 'tp'), may hold values from -0.09375 to 0.09375
- doc_lengths: int32 [16], P('groups'), parts along dimension 0, may hold values from 1 to 256, 512 in all
Outputs:
- attention_out: bfloat16 [1024, 8, 1024], P(('groups', 'fsdp'), 'tp'), parts along dimension 0
The draws below stay inside these ranges and needn't reach their ends.
There are 2 independent parts, one for each index of `groups`. The reference program is written for one: setup_inputs(seed, part) draws one part's arguments, and reference() takes and returns one part's arrays. A program takes and returns all parts, laid end to end along the dimension named above; an argument that names none is the same for every part. Nothing has to cross between parts.
Inputs may be any that keep to these rules, and one draw needn't show every extreme that they name: `doc_lengths`: the lengths sum to 512 and the longest is exactly 256.
All inputs are finite; a program needn't handle non-finite values.
Results may differ from the reference program's by a relative error of at most 0.011.
Values may be sent and summed in bfloat16 or wider, within the bound.
A program may use at most 128 MiB of HBM per device.

```python
import math
import jax
import jax.numpy as jnp
import numpy as np
from jax import lax

MODEL_WIDTH = 4096
QUERY_HEADS = 64
KEY_VALUE_HEADS = 8
HEAD_WIDTH = 128
TOK_DEV = 128
PACKED_TOKENS = 512
DOCUMENT_LENGTH = 256
NDOCS = 8


def draw_tokens(key, part):
    base_key = jax.random.fold_in(key, 0)
    values = jnp.clip(jax.random.normal(base_key, (PACKED_TOKENS, MODEL_WIDTH), jnp.float32), -4.0, 4.0)
    return values.astype(jnp.bfloat16)


def block_scale(rng, extent, pieces, smallest, top_value):
    level = 1.0
    for axis_at, shards_of in pieces:
        steps = jax.random.uniform(jax.random.fold_in(jax.random.fold_in(rng, 6), axis_at), (shards_of,), jnp.float32, smallest / len(pieces), top_value / len(pieces))
        level = level * jnp.repeat(jnp.exp(steps), extent[axis_at] // shards_of).reshape((-1,) + (1,) * (len(extent) - 1 - axis_at))
    return level


def split_up(number_of, total, bound, slope):
    loads = [(1 << 20) // math.isqrt(grade ** slope) + 1 for grade in range(2, number_of + 1)]
    surplus, given = total - bound - (number_of - 1), [1] * (number_of - 1)
    while surplus > 0:
        candidates = [i for i in range(number_of - 1) if given[i] < bound]
        mass, remaining = sum([loads[i] for i in candidates]), surplus
        for i in candidates:
            extra = min(bound - given[i], max(1, remaining * loads[i] // mass), surplus)
            given[i] = given[i] + extra
            surplus = surplus - extra
    return np.array([bound] + given)


def uneven_parts(key, number_of, total, reach, skew):
    if number_of == 2:
        one = jax.random.randint(key, (), max(1, total - reach), min(reach, total - 1) + 1)
        return jnp.stack([one, total - one])
    lengths = jnp.asarray(split_up(number_of, total, reach, skew), jnp.int32)
    couples = (number_of - 1) // 2
    giver, receiver = lengths[1:1 + 2 * couples:2], lengths[2:2 + 2 * couples:2]
    slack = jnp.minimum(giver - 1, reach - receiver)
    shifted = jax.random.randint(jax.random.fold_in(key, 1), (couples,), 0, 1 << 20) % (slack + 1)
    lengths = lengths.at[1:1 + 2 * couples:2].set(giver - shifted).at[2:2 + 2 * couples:2].set(receiver + shifted)
    return lengths[jax.random.permutation(jax.random.fold_in(key, 2), number_of)]


def noise(rng, extent, deviation, bound, cuts=(), kind=jnp.bfloat16):
    values = jax.random.normal(rng, extent, jnp.float32) * deviation
    if len(cuts) > 0:
        values = block_scale(rng, extent, cuts, -0.22, 0.18) * values
    return jnp.clip(values, min=-bound, max=bound).astype(kind)


def setup_inputs(seed: int = 0, part: int = 0) -> dict:
    keys = jax.random.split(jax.random.key(seed), 4)
    own_keys = jax.random.split(jax.random.fold_in(keys[3], part), 4)
    return {
        "tokens": draw_tokens(jax.random.fold_in(jax.random.fold_in(keys[3], part), 71), part),
        "query_key_value_weight": noise(keys[1], (MODEL_WIDTH, KEY_VALUE_HEADS, (QUERY_HEADS // KEY_VALUE_HEADS + 2) * HEAD_WIDTH), MODEL_WIDTH ** -0.5, 0.09375, ((0, 4), (1, 4))),
        "doc_lengths": uneven_parts(own_keys[2], NDOCS, PACKED_TOKENS, DOCUMENT_LENGTH, 2).astype(jnp.int32),
    }


ROPE_BASE = 500000.0
NEGATIVE = -1e30


def doc_offsets(doc_lengths, positions):
    ends = jnp.cumsum(doc_lengths).astype(jnp.int32)
    passed = (ends[None, :] <= positions[:, None]).astype(jnp.int32)
    return jnp.sum(passed * doc_lengths[None, :], axis=1).astype(jnp.int32)


def rotate(values, relative):
    half_width = values.shape[-1] // 2
    frequency = ROPE_BASE ** (-(jnp.arange(half_width, dtype=jnp.float32) / half_width))
    angles = relative[:, None] * frequency[None, :]
    angles = angles.reshape((angles.shape[0],) + (1,) * (values.ndim - 2) + (half_width,))
    cosine = jnp.cos(angles)
    sine_part = jnp.sin(angles)
    front_half = values[..., :half_width]
    back_half = values[..., half_width:]
    return jnp.concatenate([front_half * cosine - back_half * sine_part, back_half * cosine + front_half * sine_part], axis=-1)


def reference(tokens, query_key_value_weight, doc_lengths):
    positions = jnp.arange(PACKED_TOKENS, dtype=jnp.int32)
    doc_start = doc_offsets(doc_lengths, positions)
    query_group_count = QUERY_HEADS // KEY_VALUE_HEADS
    projected_rows = jnp.dot(tokens, query_key_value_weight.reshape(MODEL_WIDTH, -1), preferred_element_type=jnp.float32)
    projected_rows = projected_rows.reshape(PACKED_TOKENS, KEY_VALUE_HEADS, query_group_count + 2, HEAD_WIDTH)
    relative = (positions - doc_start).astype(jnp.float32)
    queries = rotate(projected_rows[:, :, :query_group_count], relative).astype(jnp.bfloat16)
    key_rows = rotate(projected_rows[:, :, query_group_count], relative).astype(jnp.bfloat16)
    value_rows = projected_rows[:, :, query_group_count + 1].astype(jnp.bfloat16)
    padding_width = jnp.zeros((DOCUMENT_LENGTH, KEY_VALUE_HEADS, HEAD_WIDTH), jnp.bfloat16)
    padded_keys = jnp.concatenate([padding_width, key_rows], axis=0)
    padded_values = jnp.concatenate([padding_width, value_rows], axis=0)
    window = DOCUMENT_LENGTH + TOK_DEV
    scaling = HEAD_WIDTH ** -0.5

    def one_block(block_index):
        first_row = block_index * TOK_DEV
        block_queries = lax.dynamic_slice_in_dim(queries, first_row, TOK_DEV, 0).astype(jnp.float32)
        block_keys = lax.dynamic_slice_in_dim(padded_keys, first_row, window, 0).astype(jnp.float32)
        block_values = lax.dynamic_slice_in_dim(padded_values, first_row, window, 0).astype(jnp.float32)
        block_positions = lax.dynamic_slice_in_dim(positions, first_row, TOK_DEV, 0)
        block_starts = lax.dynamic_slice_in_dim(doc_start, first_row, TOK_DEV, 0)
        key_index = first_row - DOCUMENT_LENGTH + jnp.arange(window, dtype=jnp.int32)
        scores = jnp.einsum("thgd,khd->hgtk", block_queries, block_keys) * scaling
        allowed = (key_index[None, :] >= block_starts[:, None]) & (key_index[None, :] <= block_positions[:, None])
        scores = jnp.where(allowed, scores, NEGATIVE)
        row_max = jnp.max(scores, axis=-1, keepdims=True)
        unscaled = jnp.where(allowed, jnp.exp(scores - row_max), 0.0)
        weight_sum = jnp.sum(unscaled, axis=-1)
        weights = lax.optimization_barrier(unscaled.astype(jnp.bfloat16)).astype(jnp.float32)
        mixed_rows = jnp.einsum("hgtk,khd->thgd", weights, block_values)
        return (mixed_rows / jnp.transpose(weight_sum, (2, 0, 1))[..., None]).astype(jnp.bfloat16)

    block_list = lax.map(one_block, jnp.arange(PACKED_TOKENS // TOK_DEV, dtype=jnp.int32))
    return block_list.reshape(PACKED_TOKENS, KEY_VALUE_HEADS, query_group_count * HEAD_WIDTH)
```

```python
import functools

import jax
import jax.numpy as jnp
import numpy as np
from jax import lax
from jax.experimental import pallas as pl
from jax.experimental.pallas import tpu as pltpu
from jax.sharding import PartitionSpec as P

HEAD_WIDTH = 128
ROPE_BASE = 500000.0
NEGATIVE = -1e30
LEVELS = 32000.0
MESH = pl.DeviceIdType.MESH


def dot(a, b):
    return jnp.dot(a, b, preferred_element_type=jnp.float32)


def dot_t(a, b):
    return lax.dot_general(a, b, (((1,), (1,)), ((), ())), preferred_element_type=jnp.float32)


def kernel(
    n, ranks, span, lengths_ref, freq_ref, tokens_ref, weight_ref, out_ref,
    raw, weights, x_own, x_in, part_out, part_in, scale_out, scale_in, own, window,
    raw_sem, x_sem, tok_send, tok_recv, share_send, share_recv,
    part_send, part_recv, scale_send, scale_recv, kv_send, kv_recv,
):
    me = lax.axis_index("fsdp")
    rank = lax.axis_index("tp")
    tok = tokens_ref.shape[0]
    rows, heads, width = weight_ref.shape
    group = width // HEAD_WIDTH - 2
    qw = group * HEAD_WIDTH
    kvw = heads * 2 * HEAD_WIDTH
    chunks = [(0, kvw)] + [(kvw + h * qw, qw) for h in range(heads)]
    count = len(chunks)
    order = list(range(1, n))
    relayed = n == 4
    inner = (me == 1) | (me == 2)

    def peer(s):
        return lax.rem(me + s, n)

    def target(s):
        if relayed and s is order[1]:
            return jnp.where(inner, jnp.where(me == 1, 3, 0), jnp.where(me == 0, 1, 2))
        return peer(s)

    block = 128
    blocks = rows // block
    raw_copies = [
        pltpu.make_async_copy(
            weight_ref.at[pl.ds(b * block, block)], raw.at[pl.ds(b * block, block)], raw_sem.at[b]
        )
        for b in range(blocks)
    ]
    for copy in raw_copies:
        copy.start()
    own_copy = pltpu.make_async_copy(
        tokens_ref.at[:, pl.ds(pl.multiple_of(me * rows, 128), rows)], x_own, x_sem
    )
    own_copy.start()
    window[...] = jnp.zeros_like(window)

    barrier = pltpu.get_barrier_semaphore()
    for s in range(1, n):
        pl.semaphore_signal(barrier, inc=1, device_id={"fsdp": peer(s)}, device_id_type=MESH)
    for d in range(1, ranks):
        pl.semaphore_signal(
            barrier, inc=1, device_id={"tp": lax.rem(rank + d, ranks)}, device_id_type=MESH
        )
    pl.semaphore_wait(barrier, n - 1 + ranks - 1)

    sub = tok // ranks
    share = pl.ds(pl.multiple_of(rank * sub, sub), sub)
    tok_copies = {}
    for s in order:
        tok_copies[s] = pltpu.make_async_remote_copy(
            src_ref=tokens_ref.at[share, pl.ds(pl.multiple_of(peer(s) * rows, 128), rows)],
            dst_ref=x_in.at[s - 1, share],
            send_sem=tok_send.at[s - 1],
            recv_sem=tok_recv.at[s - 1],
            device_id={"fsdp": peer(s)},
            device_id_type=MESH,
        )
        tok_copies[s].start()
    share_copies = {}

    def pass_round():
        for s in order:
            tok_copies[s].wait_recv()
            for d in range(1, ranks):
                share_copies[s, d] = pltpu.make_async_remote_copy(
                    src_ref=x_in.at[s - 1, share],
                    dst_ref=x_in.at[s - 1, share],
                    send_sem=share_send.at[s - 1, d - 1],
                    recv_sem=share_recv.at[s - 1, d - 1],
                    device_id={"tp": lax.rem(rank + d, ranks)},
                    device_id_type=MESH,
                )
                share_copies[s, d].start()

    mixed = heads * block
    to_row = lax.broadcasted_iota(jnp.int32, (mixed, mixed), 0)
    from_row = lax.broadcasted_iota(jnp.int32, (mixed, mixed), 1)
    pick = (from_row == (to_row % block) * heads + to_row // block).astype(jnp.bfloat16)
    for b in range(blocks):
        if b == blocks // 2:
            pass_round()
        raw_copies[b].wait()
        at = pl.ds(b * block, block)
        piece = raw[at].reshape(mixed, width)
        if heads > 1:
            piece = dot(pick, piece).astype(jnp.bfloat16)
        for h in range(heads):
            part = piece[h * block : (h + 1) * block]
            weights[at, pl.ds(h * 2 * HEAD_WIDTH, 2 * HEAD_WIDTH)] = part[:, qw:]
            weights[at, pl.ds(kvw + h * qw, qw)] = part[:, :qw]
    for s in order:
        for d in range(1, ranks):
            share_copies[s, d].wait_recv()

    def copies(c, s):
        start, size = chunks[c]
        at = pl.ds(start, size)
        slot = s - 1
        common = dict(device_id={"fsdp": target(s)}, device_id_type=MESH)
        return (
            pltpu.make_async_remote_copy(
                src_ref=part_out.at[slot, :, at],
                dst_ref=part_in.at[slot, :, at],
                send_sem=part_send.at[c, slot],
                recv_sem=part_recv.at[c, slot],
                **common,
            ),
            pltpu.make_async_remote_copy(
                src_ref=scale_out.at[slot, :, at],
                dst_ref=scale_in.at[slot, :, at],
                send_sem=scale_send.at[c, slot],
                recv_sem=scale_recv.at[c, slot],
                **common,
            ),
        )

    def received(slot, at):
        return part_in[slot, :, at].astype(jnp.int32).astype(jnp.float32) * scale_in[slot, :, at]

    def wait_recv(c, s):
        for copy in copies(c, s):
            copy.wait_recv()

    def send(c, s, relay):
        at = pl.ds(*chunks[c])
        value = dot(x_in[n - s - 1], weights[:, at])
        if relay:
            wait_recv(c, order[1])
            value = value + received(1, at) * jnp.where(inner, 1.0, 0.0)
        largest = jnp.maximum(jnp.max(jnp.abs(value), axis=0, keepdims=True), 1e-30)
        coded = jnp.round(value * (LEVELS / largest))
        part_out[s - 1, :, at] = coded.astype(jnp.int32).astype(jnp.int16)
        scale_out[s - 1, :, at] = largest * (1.0 / LEVELS)
        for copy in copies(c, s):
            copy.start()

    def own_part():
        own_copy.wait()
        for start, size in chunks:
            at = pl.ds(start, size)
            own[:, at] = dot(x_own[...], weights[:, at])

    if relayed:
        away = jnp.where(me == 2, 1, 3)
        across = 4 - away
        for c in range(count):
            send(c, order[1], False)
            send(c, away, False)
            if c == 1:
                own_part()
            if c >= 1:
                send(c - 1, across, True)
        if count == 1:
            own_part()
        send(count - 1, across, True)
    else:
        for c in range(count):
            for s in order:
                send(c, s, False)
        own_part()

    position = me * tok + lax.broadcasted_iota(jnp.int32, (tok, HEAD_WIDTH), 0)
    lane = lax.broadcasted_iota(jnp.int32, (tok, HEAD_WIDTH), 1)
    doc_start = jnp.zeros((tok, HEAD_WIDTH), jnp.int32)
    end = jnp.int32(0)
    for d in range(lengths_ref.shape[0]):
        length = lengths_ref[d]
        end = end + length
        doc_start = doc_start + jnp.where(position >= end, length, 0)
    angle = (position - doc_start).astype(jnp.float32) * freq_ref[...]
    cosine = jnp.cos(angle)
    sine = jnp.where(lane < HEAD_WIDTH // 2, -jnp.sin(angle), jnp.sin(angle))
    biases = []
    for w in range(span + 1):
        for half in range(tok // 128):
            key = (me - span + w) * tok + half * 128 + lane
            allowed = (key >= doc_start) & (key <= position)
            biases.append(jnp.where(allowed, 0.0, NEGATIVE))
    bias = jnp.concatenate(biases, axis=1)

    def rotate(u):
        return (u * cosine + pltpu.roll(u, HEAD_WIDTH // 2, 1) * sine).astype(jnp.bfloat16)

    def arrive(c):
        for s in order:
            if not (relayed and s is order[1]):
                wait_recv(c, s)

    def total(at):
        value = own[:, at]
        for s in order:
            term = received(s - 1, at)
            if relayed and s is order[1]:
                term = term * jnp.where(inner, 0.0, 1.0)
            value = value + term
        return value

    arrive(0)
    mine = pl.ds(span * tok, tok)
    for h in range(heads):
        key_at = pl.ds(2 * h * HEAD_WIDTH, HEAD_WIDTH)
        value_at = pl.ds((2 * h + 1) * HEAD_WIDTH, HEAD_WIDTH)
        window[mine, key_at] = rotate(total(key_at))
        window[mine, value_at] = total(value_at).astype(jnp.bfloat16)
    kv_copies = []
    for j in range(1, span + 1):
        copy = pltpu.make_async_remote_copy(
            src_ref=window.at[mine],
            dst_ref=window.at[pl.ds((span - j) * tok, tok)],
            send_sem=kv_send.at[j - 1],
            recv_sem=kv_recv.at[j - 1],
            device_id={"fsdp": peer(j)},
            device_id_type=MESH,
        )
        kv_copies.append(copy)

        @pl.when(me + j < n)
        def _():
            copy.start()

    for j in range(1, span + 1):

        @pl.when(me >= j)
        def _():
            kv_copies[j - 1].wait_recv()

    scaling = HEAD_WIDTH**-0.5
    for h in range(heads):
        arrive(h + 1)
        keys = window[:, pl.ds(2 * h * HEAD_WIDTH, HEAD_WIDTH)]
        values = window[:, pl.ds((2 * h + 1) * HEAD_WIDTH, HEAD_WIDTH)]
        for g in range(group):
            query = rotate(total(pl.ds(kvw + h * qw + g * HEAD_WIDTH, HEAD_WIDTH)))
            scores = dot_t(query, keys) * scaling + bias
            unscaled = jnp.exp(scores - jnp.max(scores, axis=1, keepdims=True))
            weight_sum = jnp.sum(unscaled, axis=1, keepdims=True)
            mixed_rows = dot(unscaled.astype(jnp.bfloat16), values)
            out_ref[:, pl.ds(h * qw + g * HEAD_WIDTH, HEAD_WIDTH)] = (
                mixed_rows / weight_sum
            ).astype(jnp.bfloat16)

    for s in order:
        tok_copies[s].wait_send()
        for d in range(1, ranks):
            share_copies[s, d].wait_send()
        for c in range(count):
            for copy in copies(c, s):
                copy.wait_send()
    for j in range(1, span + 1):

        @pl.when(me + j < n)
        def _():
            kv_copies[j - 1].wait_send()


def on_device(n, ranks, tokens, weight, doc_lengths):
    tok, model = tokens.shape
    rows, heads, width = weight.shape
    span = min(16, n // 2)
    group = width // HEAD_WIDTH - 2
    half = HEAD_WIDTH // 2
    frequency = np.float32(ROPE_BASE) ** (-(np.arange(half, dtype=np.float32) / np.float32(half)))
    freq = jnp.asarray(np.concatenate([frequency, frequency])[None, :].astype(np.float32))
    bf16 = jnp.bfloat16
    out = pl.pallas_call(
        functools.partial(kernel, n, ranks, span),
        out_shape=jax.ShapeDtypeStruct((tok, heads * group * HEAD_WIDTH), bf16),
        in_specs=[
            pl.BlockSpec(memory_space=pltpu.SMEM),
            pl.BlockSpec(memory_space=pltpu.VMEM),
            pl.BlockSpec(memory_space=pl.ANY),
            pl.BlockSpec(memory_space=pl.ANY),
        ],
        out_specs=pl.BlockSpec(memory_space=pltpu.VMEM),
        scratch_shapes=[
            pltpu.VMEM((rows, heads, width), bf16),
            pltpu.VMEM((rows, heads * width), bf16),
            pltpu.VMEM((tok, rows), bf16),
            pltpu.VMEM((n - 1, tok, rows), bf16),
            pltpu.VMEM((n - 1, tok, heads * width), jnp.int16),
            pltpu.VMEM((n - 1, tok, heads * width), jnp.int16),
            pltpu.VMEM((n - 1, 1, heads * width), jnp.float32),
            pltpu.VMEM((n - 1, 1, heads * width), jnp.float32),
            pltpu.VMEM((tok, heads * width), jnp.float32),
            pltpu.VMEM(((span + 1) * tok, heads * 2 * HEAD_WIDTH), bf16),
            pltpu.SemaphoreType.DMA((rows // 128,)),
            pltpu.SemaphoreType.DMA,
            pltpu.SemaphoreType.DMA((n - 1,)),
            pltpu.SemaphoreType.DMA((n - 1,)),
            pltpu.SemaphoreType.DMA((n - 1, ranks - 1)),
            pltpu.SemaphoreType.DMA((n - 1, ranks - 1)),
            pltpu.SemaphoreType.DMA((heads + 1, n - 1)),
            pltpu.SemaphoreType.DMA((heads + 1, n - 1)),
            pltpu.SemaphoreType.DMA((heads + 1, n - 1)),
            pltpu.SemaphoreType.DMA((heads + 1, n - 1)),
            pltpu.SemaphoreType.DMA((span,)),
            pltpu.SemaphoreType.DMA((span,)),
        ],
        compiler_params=pltpu.CompilerParams(
            collective_id=0, has_side_effects=True, vmem_limit_bytes=56 * 2**20
        ),
    )(doc_lengths, freq, tokens, weight)
    return out.reshape(tok, heads, group * HEAD_WIDTH)


def solution(mesh):
    return jax.shard_map(
        functools.partial(on_device, mesh.shape["fsdp"], mesh.shape["tp"]),
        mesh=mesh,
        in_specs=(P(("groups", "fsdp"), None), P("fsdp", "tp", None), P("groups")),
        out_specs=P(("groups", "fsdp"), "tp", None),
        check_vma=False,
    )
```

```python
import functools

import jax
import jax.numpy as jnp
import numpy as np
from jax import lax
from jax.experimental import pallas as pl
from jax.experimental.pallas import tpu as pltpu
from jax.sharding import PartitionSpec as P

HEAD_WIDTH = 128
ROPE_BASE = 500000.0
NEGATIVE = -1e30
LEVELS = 32000.0
CUTS = 1
MESH = pl.DeviceIdType.MESH


def dot(a, b):
    return jnp.dot(a, b, preferred_element_type=jnp.float32)


def dot_t(a, b):
    return lax.dot_general(a, b, (((1,), (1,)), ((), ())), preferred_element_type=jnp.float32)


def kernel(
    n, ranks, span, lengths_ref, freq_ref, tokens_ref, weight_ref, out_ref,
    raw, weights, x_own, x_in, part_out, part_in, scale_out, scale_in, own, window,
    raw_sem, x_sem, tok_send, tok_recv, share_send, share_recv,
    part_send, part_recv, scale_send, scale_recv, kv_send, kv_recv,
):
    me = lax.axis_index("fsdp")
    rank = lax.axis_index("tp")
    tok = tokens_ref.shape[0]
    rows, heads, width = weight_ref.shape
    group = width // HEAD_WIDTH - 2
    qw = group * HEAD_WIDTH
    kvw = heads * 2 * HEAD_WIDTH
    cut = qw // CUTS
    chunks = [(0, kvw)] + [(kvw + q * cut, cut) for q in range(heads * CUTS)]
    count = len(chunks)
    relayed = n == 4
    order = [2, 1, 3] if relayed else list(range(1, n))
    inner = (me == 1) | (me == 2)

    def peer(s):
        return lax.rem(me + s, n)

    def target(s):
        if relayed and s is order[0]:
            return jnp.where(inner, jnp.where(me == 1, 3, 0), jnp.where(me == 0, 1, 2))
        return peer(s)

    block = 128
    blocks = rows // block
    parts = [(pl.ds(0, rows), pl.ds(qw, 2 * HEAD_WIDTH))]
    parts += [(pl.ds(b * block, block), pl.ds(0, qw)) for b in range(blocks)]
    raw_copies = [
        pltpu.make_async_copy(
            weight_ref.at[r, :, columns], raw.at[r, :, columns], raw_sem.at[i]
        )
        for i, (r, columns) in enumerate(parts)
    ]
    for copy in raw_copies:
        copy.start()
    own_copy = pltpu.make_async_copy(
        tokens_ref.at[:, pl.ds(pl.multiple_of(me * rows, 128), rows)], x_own, x_sem
    )
    own_copy.start()
    window[...] = jnp.zeros_like(window)

    barrier = pltpu.get_barrier_semaphore()
    for s in range(1, n):
        pl.semaphore_signal(barrier, inc=1, device_id={"fsdp": peer(s)}, device_id_type=MESH)
    for d in range(1, ranks):
        pl.semaphore_signal(
            barrier, inc=1, device_id={"tp": lax.rem(rank + d, ranks)}, device_id_type=MESH
        )
    pl.semaphore_wait(barrier, n - 1 + ranks - 1)

    sub = tok // ranks
    share = pl.ds(pl.multiple_of(rank * sub, sub), sub)
    tok_copies = {}
    for s in order:
        tok_copies[s] = pltpu.make_async_remote_copy(
            src_ref=tokens_ref.at[share, pl.ds(pl.multiple_of(peer(s) * rows, 128), rows)],
            dst_ref=x_in.at[s - 1, share],
            send_sem=tok_send.at[s - 1],
            recv_sem=tok_recv.at[s - 1],
            device_id={"fsdp": peer(s)},
            device_id_type=MESH,
        )
        tok_copies[s].start()

    def share_copy(s, d):
        return pltpu.make_async_remote_copy(
            src_ref=x_in.at[s - 1, share],
            dst_ref=x_in.at[s - 1, share],
            send_sem=share_send.at[s - 1, d - 1],
            recv_sem=share_recv.at[s - 1, d - 1],
            device_id={"tp": lax.rem(rank + d, ranks)},
            device_id_type=MESH,
        )

    def pass_round():
        for s in order:
            tok_copies[s].wait_recv()
            for d in range(1, ranks):
                share_copy(s, d).start()

    mixed = heads * block
    to_row = lax.broadcasted_iota(jnp.int32, (mixed, mixed), 0)
    from_row = lax.broadcasted_iota(jnp.int32, (mixed, mixed), 1)
    pick = (from_row == (to_row % block) * heads + to_row // block).astype(jnp.bfloat16)

    def by_head(b, columns, start, size):
        at = pl.ds(b * block, block)
        piece = raw[at, :, columns].reshape(mixed, size)
        if heads > 1:
            piece = dot(pick, piece).astype(jnp.bfloat16)
        for h in range(heads):
            weights[at, pl.ds(start + h * size, size)] = piece[h * block : (h + 1) * block]

    raw_copies[0].wait()
    for b in range(blocks):
        by_head(b, parts[0][1], 0, 2 * HEAD_WIDTH)
    for b in range(blocks):
        if b == blocks // 2:
            pass_round()
        raw_copies[b + 1].wait()
        by_head(b, parts[1][1], kvw, qw)

    def copies(c, s):
        start, size = chunks[c]
        at = pl.ds(start, size)
        slot = s - 1
        common = dict(device_id={"fsdp": target(s)}, device_id_type=MESH)
        return (
            pltpu.make_async_remote_copy(
                src_ref=part_out.at[slot, :, at],
                dst_ref=part_in.at[slot, :, at],
                send_sem=part_send.at[c, slot],
                recv_sem=part_recv.at[c, slot],
                **common,
            ),
            pltpu.make_async_remote_copy(
                src_ref=scale_out.at[slot, :, at],
                dst_ref=scale_in.at[slot, :, at],
                send_sem=scale_send.at[c, slot],
                recv_sem=scale_recv.at[c, slot],
                **common,
            ),
        )

    def received(slot, at):
        return part_in[slot, :, at].astype(jnp.int32).astype(jnp.float32) * scale_in[slot, :, at]

    def wait_recv(c, s):
        for copy in copies(c, s):
            copy.wait_recv()

    def send(c, s, relay):
        at = pl.ds(*chunks[c])
        if c == 0:
            for d in range(1, ranks):
                share_copy(n - s, d).wait_recv()
        value = dot(x_in[n - s - 1], weights[:, at])
        if relay:
            wait_recv(c, order[0])
            value = value + received(1, at) * jnp.where(inner, 1.0, 0.0)
        largest = jnp.maximum(jnp.max(jnp.abs(value), axis=0, keepdims=True), 1e-30)
        coded = jnp.round(value * (LEVELS / largest))
        part_out[s - 1, :, at] = coded.astype(jnp.int32).astype(jnp.int16)
        scale_out[s - 1, :, at] = largest * (1.0 / LEVELS)
        for copy in copies(c, s):
            copy.start()

    def own_part():
        own_copy.wait()
        for start, size in chunks:
            at = pl.ds(start, size)
            own[:, at] = dot(x_own[...], weights[:, at])

    if relayed:
        away = jnp.where(me == 2, 1, 3)
        across = 4 - away
        for c in range(count):
            send(c, order[0], False)
            send(c, away, False)
            if c == 1:
                own_part()
            if c >= 1:
                send(c - 1, across, True)
        if count == 1:
            own_part()
        send(count - 1, across, True)
    else:
        for c in range(count):
            for s in order:
                send(c, s, False)
        own_part()

    position = me * tok + lax.broadcasted_iota(jnp.int32, (tok, HEAD_WIDTH), 0)
    lane = lax.broadcasted_iota(jnp.int32, (tok, HEAD_WIDTH), 1)
    doc_start = jnp.zeros((tok, HEAD_WIDTH), jnp.int32)
    end = jnp.int32(0)
    for d in range(lengths_ref.shape[0]):
        length = lengths_ref[d]
        end = end + length
        doc_start = doc_start + jnp.where(position >= end, length, 0)
    angle = (position - doc_start).astype(jnp.float32) * freq_ref[...]
    cosine = jnp.cos(angle)
    sine = jnp.where(lane < HEAD_WIDTH // 2, -jnp.sin(angle), jnp.sin(angle))
    biases = []
    for w in range(span + 1):
        for half in range(tok // 128):
            key = (me - span + w) * tok + half * 128 + lane
            allowed = (key >= doc_start) & (key <= position)
            biases.append(jnp.where(allowed, 0.0, NEGATIVE))
    bias = jnp.concatenate(biases, axis=1)

    def rotate(u):
        return (u * cosine + pltpu.roll(u, HEAD_WIDTH // 2, 1) * sine).astype(jnp.bfloat16)

    def arrive(c):
        for s in order:
            if not (relayed and s is order[0]):
                wait_recv(c, s)

    def total(at):
        value = own[:, at]
        for s in order:
            term = received(s - 1, at)
            if relayed and s is order[0]:
                term = term * jnp.where(inner, 0.0, 1.0)
            value = value + term
        return value

    arrive(0)
    mine = pl.ds(span * tok, tok)
    for h in range(heads):
        key_at = pl.ds(2 * h * HEAD_WIDTH, HEAD_WIDTH)
        value_at = pl.ds((2 * h + 1) * HEAD_WIDTH, HEAD_WIDTH)
        window[mine, key_at] = rotate(total(key_at))
        window[mine, value_at] = total(value_at).astype(jnp.bfloat16)
    kv_copies = []
    for j in range(1, span + 1):
        copy = pltpu.make_async_remote_copy(
            src_ref=window.at[mine],
            dst_ref=window.at[pl.ds((span - j) * tok, tok)],
            send_sem=kv_send.at[j - 1],
            recv_sem=kv_recv.at[j - 1],
            device_id={"fsdp": peer(j)},
            device_id_type=MESH,
        )
        kv_copies.append(copy)

        @pl.when(me + j < n)
        def _():
            copy.start()

    for j in range(1, span + 1):

        @pl.when(me >= j)
        def _():
            kv_copies[j - 1].wait_recv()

    scaling = HEAD_WIDTH**-0.5
    for h in range(heads):
        keys = window[:, pl.ds(2 * h * HEAD_WIDTH, HEAD_WIDTH)]
        values = window[:, pl.ds((2 * h + 1) * HEAD_WIDTH, HEAD_WIDTH)]
        for g in range(group):
            if g % (group // CUTS) == 0:
                arrive(1 + (h * group + g) // (group // CUTS))
            query = rotate(total(pl.ds(kvw + h * qw + g * HEAD_WIDTH, HEAD_WIDTH)))
            scores = dot_t(query, keys) * scaling + bias
            unscaled = jnp.exp(scores - jnp.max(scores, axis=1, keepdims=True))
            weight_sum = jnp.sum(unscaled, axis=1, keepdims=True)
            mixed_rows = dot(unscaled.astype(jnp.bfloat16), values)
            out_ref[:, pl.ds(h * qw + g * HEAD_WIDTH, HEAD_WIDTH)] = (
                mixed_rows / weight_sum
            ).astype(jnp.bfloat16)

    for s in order:
        tok_copies[s].wait_send()
        for d in range(1, ranks):
            share_copy(s, d).wait_send()
        for c in range(count):
            for copy in copies(c, s):
                copy.wait_send()
    for j in range(1, span + 1):

        @pl.when(me + j < n)
        def _():
            kv_copies[j - 1].wait_send()


def on_device(n, ranks, tokens, weight, doc_lengths):
    tok, model = tokens.shape
    rows, heads, width = weight.shape
    span = min(16, n // 2)
    group = width // HEAD_WIDTH - 2
    half = HEAD_WIDTH // 2
    frequency = np.float32(ROPE_BASE) ** (-(np.arange(half, dtype=np.float32) / np.float32(half)))
    freq = jnp.asarray(np.concatenate([frequency, frequency])[None, :].astype(np.float32))
    bf16 = jnp.bfloat16
    out = pl.pallas_call(
        functools.partial(kernel, n, ranks, span),
        out_shape=jax.ShapeDtypeStruct((tok, heads * group * HEAD_WIDTH), bf16),
        in_specs=[
            pl.BlockSpec(memory_space=pltpu.SMEM),
            pl.BlockSpec(memory_space=pltpu.VMEM),
            pl.BlockSpec(memory_space=pl.ANY),
            pl.BlockSpec(memory_space=pl.ANY),
        ],
        out_specs=pl.BlockSpec(memory_space=pltpu.VMEM),
        scratch_shapes=[
            pltpu.VMEM((rows, heads, width), bf16),
            pltpu.VMEM((rows, heads * width), bf16),
            pltpu.VMEM((tok, rows), bf16),
            pltpu.VMEM((n - 1, tok, rows), bf16),
            pltpu.VMEM((n - 1, tok, heads * width), jnp.int16),
            pltpu.VMEM((n - 1, tok, heads * width), jnp.int16),
            pltpu.VMEM((n - 1, 1, heads * width), jnp.float32),
            pltpu.VMEM((n - 1, 1, heads * width), jnp.float32),
            pltpu.VMEM((tok, heads * width), jnp.float32),
            pltpu.VMEM(((span + 1) * tok, heads * 2 * HEAD_WIDTH), bf16),
            pltpu.SemaphoreType.DMA((rows // 128 + 1,)),
            pltpu.SemaphoreType.DMA,
            pltpu.SemaphoreType.DMA((n - 1,)),
            pltpu.SemaphoreType.DMA((n - 1,)),
            pltpu.SemaphoreType.DMA((n - 1, ranks - 1)),
            pltpu.SemaphoreType.DMA((n - 1, ranks - 1)),
            pltpu.SemaphoreType.DMA((heads * CUTS + 1, n - 1)),
            pltpu.SemaphoreType.DMA((heads * CUTS + 1, n - 1)),
            pltpu.SemaphoreType.DMA((heads * CUTS + 1, n - 1)),
            pltpu.SemaphoreType.DMA((heads * CUTS + 1, n - 1)),
            pltpu.SemaphoreType.DMA((span,)),
            pltpu.SemaphoreType.DMA((span,)),
        ],
        compiler_params=pltpu.CompilerParams(
            collective_id=0, has_side_effects=True, vmem_limit_bytes=56 * 2**20
        ),
    )(doc_lengths, freq, tokens, weight)
    return out.reshape(tok, heads, group * HEAD_WIDTH)


def solution(mesh):
    return jax.shard_map(
        functools.partial(on_device, mesh.shape["fsdp"], mesh.shape["tp"]),
        mesh=mesh,
        in_specs=(P(("groups", "fsdp"), None), P("fsdp", "tp", None), P("groups")),
        out_specs=P(("groups", "fsdp"), "tp", None),
        check_vma=False,
    )
```
